256 devices in a mesh: rows: 16 (over y, z_lo), pairs: 16 (over x, z_hi, core).
Axes of the slice: x: 4, y: 4, z: 8 (z_hi: 2, z_lo: 4; z = z_hi * 4 + z_lo), core: 2. Of those that a mesh axis runs over, the one named last changes fastest.
Arguments:
- snapshots: float32 [8192, 8192], P('rows', 'pairs')
- pairing: int32 [5, 16, 8], P(None, 'pairs'), may hold values from 0 to 7, each once within a row
Outputs:
- rotated: float32 [8192, 8192], P('rows', 'pairs')
The draws below stay inside these ranges and needn't reach their ends.
Inputs may be any that keep to these rules, and one draw needn't show every extreme that they name: Each row pairing[r, g, :] is a permutation of the slots 0 .. 7.
All inputs are finite; a program needn't handle non-finite values. Where the reference program divides by a largest or mean magnitude, that divisor is 1e-20 or more.
Results may differ from the reference program's by a relative error of at most 0.00024.
Values sent between devices are 32-bit elements; how exact they have to be, the bound alone decides.
No kernel may reach another device: no remote copies, remote signals or barrier semaphores. Data moves between devices by JAX's collectives and lax.ppermute only.
A program may use at most 64 MiB of HBM per device.

```python
import math
import jax
import jax.numpy as jnp
from jax import lax

BLK = 64
PAIRS_DEV = 4
ROUNDS = 5
NS_STEPS = 6
M = 8192
NCOLS = 8192
N_PAIRS = 16


def draw_snapshots(key, part):
    key = jax.random.fold_in(key, 7)
    key_noise = jax.random.fold_in(key, 0)
    key_row = jax.random.fold_in(key, 1)
    key_col = jax.random.fold_in(key, 2)
    key_mode = jax.random.fold_in(key, 4)
    key_coef = jax.random.fold_in(key, 5)
    ramp = jnp.arange(M, dtype=jnp.float32)[:, None] / M - 0.5
    modes = jax.random.normal(key_mode, (4, M), jnp.float32)
    coefs = jax.random.normal(key_coef, (4, NCOLS), jnp.float32)
    noise = jax.random.normal(key_noise, (M, NCOLS), jnp.float32)
    slope = math.log(3.0)
    weights = [0.9, 0.6, 0.4, 0.25]
    field = noise
    for index in range(4):
        field = field + weights[index] * modes[index][:, None] * coefs[index][None, :]
    row_scale = jnp.exp(jax.random.uniform(key_row, (M, 1), jnp.float32, math.log(0.3), math.log(3.0)) + slope * ramp)
    col_scale = jnp.exp(jax.random.uniform(key_col, (1, NCOLS), jnp.float32, math.log(0.3), math.log(3.0)))
    return field * row_scale * col_scale


def setup_inputs(seed: int = 0) -> dict:
    seeds = jax.random.split(jax.random.key(seed), 3)
    snapshots = draw_snapshots(jax.random.fold_in(seeds[2], 71), 0)
    pairing = jax.vmap(lambda own: jax.random.permutation(own, 2 * PAIRS_DEV))(jax.random.split(seeds[1], ROUNDS * N_PAIRS)).reshape((ROUNDS, N_PAIRS, 2 * PAIRS_DEV)).astype(jnp.int32)
    return {"snapshots": snapshots, "pairing": pairing}


def make_rotation(gram):
    width = gram.shape[-1]
    eye = jnp.eye(width, dtype=jnp.float32)
    diag = jnp.diagonal(gram, axis1=1, axis2=2) + 1e-06
    scale = lax.rsqrt(diag)
    unit = gram * scale[:, :, None] * scale[:, None, :]
    bound = lax.optimization_barrier(jnp.max(lax.optimization_barrier(jnp.sum(jnp.abs(unit), axis=2)), axis=1))
    ymat = unit / bound[:, None, None]
    zmat = jnp.broadcast_to(eye, unit.shape)
    for step in range(NS_STEPS):
        prod = 1.5 * eye - 0.5 * jnp.einsum('kab,kbc->kac', zmat, ymat, precision=lax.Precision.HIGHEST)
        ymat = jnp.einsum('kab,kbc->kac', ymat, prod, precision=lax.Precision.HIGHEST)
        zmat = jnp.einsum('kab,kbc->kac', prod, zmat, precision=lax.Precision.HIGHEST)
    return zmat * scale[:, :, None] * jnp.sqrt(diag)[:, None, :] * lax.rsqrt(bound)[:, None, None]

def group_round(operands):
    block, order = operands
    rows_all = block.shape[0]
    width = block.shape[2]
    pair_cols = block[:, order, :].reshape(rows_all, order.shape[0] // 2, 2 * width)
    gram = jnp.einsum('mka,mkb->kab', pair_cols, pair_cols, precision=lax.Precision.HIGHEST)
    rotation = make_rotation(gram)
    fresh = jnp.einsum('mka,kab->mkb', pair_cols, rotation, precision=lax.Precision.HIGHEST)
    return (fresh[:, :, :width], fresh[:, :, width:])

def reference(snapshots, pairing):
    groups = pairing.shape[1]
    slots = pairing.shape[2]
    current = snapshots.reshape(M, groups, slots, BLK).transpose(1, 0, 2, 3)
    for step in range(ROUNDS):
        kept, moving = lax.map(group_round, (current, pairing[step]))
        arrived = jnp.roll(moving, 1, axis=0)
        current = jnp.stack([kept, arrived], axis=3).reshape(groups, M, slots, BLK)
    return current.transpose(1, 0, 2, 3).reshape(M, groups * slots * BLK)
```

```python
import jax
import jax.numpy as jnp
from jax import lax
from jax.experimental import pallas as pl
from jax.experimental.pallas import tpu as pltpu
from jax.sharding import PartitionSpec as P

BLK = 64
WIDE = 2 * BLK
ROUNDS = 5
NS_STEPS = 6

VMEM = pl.BlockSpec(memory_space=pltpu.VMEM)
SMEM = pl.BlockSpec(memory_space=pltpu.SMEM)


def halves(x):
    high = x.astype(jnp.bfloat16)
    low = (x - high.astype(jnp.float32)).astype(jnp.bfloat16)
    return high, low


def left_form(x):
    return jnp.concatenate(halves(x), axis=1)


def right_form(x):
    row = jnp.concatenate(halves(x), axis=1)
    return jnp.concatenate([row, row], axis=0)


def folded(left, right):
    out = jnp.dot(left, right, preferred_element_type=jnp.float32)
    half = out.shape[1] // 2
    return out[:, :half] + out[:, half:]


def spread(kept_ref, arrived_ref, high_ref, low_ref):
    for k in range(kept_ref.shape[0]):
        for side, ref in enumerate((kept_ref, arrived_ref)):
            high, low = halves(ref[k])
            high_ref[2 * k + side] = high
            low_ref[2 * k + side] = low


def gram_kernel(order_ref, kept_ref, arrived_ref, gram_ref, high_ref, low_ref):
    spread(kept_ref, arrived_ref, high_ref, low_ref)
    for k in range(kept_ref.shape[0]):
        first, second = order_ref[2 * k], order_ref[2 * k + 1]
        both = jnp.concatenate(
            [high_ref[first], high_ref[second], low_ref[first], low_ref[second]], axis=0
        )
        out = lax.dot_general(
            both, both, (((1,), (1,)), ((), ())), preferred_element_type=jnp.float32
        )
        out = out[:WIDE] + out[WIDE:]
        gram_ref[k] = out[:, :WIDE] + out[:, WIDE:]


def total_kernel(parts_ref, out_ref):
    total = jnp.sum(parts_ref[...], axis=0)
    for i in range(out_ref.shape[0]):
        out_ref[i] = total


def turned(gram):
    row = lax.broadcasted_iota(jnp.int32, (WIDE, WIDE), 0)
    col = lax.broadcasted_iota(jnp.int32, (WIDE, WIDE), 1)
    on_diag = row == col
    eye = on_diag.astype(jnp.float32)
    ymats, zmats, outer = [], [], []
    for g in gram:
        only = jnp.where(on_diag, g, 0.0)
        diag_col = jnp.sum(only, axis=1, keepdims=True) + 1e-06
        diag_row = jnp.sum(only, axis=0, keepdims=True) + 1e-06
        scale_row = lax.rsqrt(diag_row)
        unit = g * lax.rsqrt(diag_col) * scale_row
        bound = jnp.max(jnp.sum(jnp.abs(unit), axis=1, keepdims=True), axis=0, keepdims=True)
        ymats.append(unit / bound)
        outer.append((jnp.sqrt(diag_col) * lax.rsqrt(bound), scale_row))
    for step in range(NS_STEPS):
        if step == 0:
            prods = [1.5 * eye - 0.5 * y for y in ymats]
            ymats = [folded(left_form(y), right_form(p)) for y, p in zip(ymats, prods)]
            zmats = prods
            continue
        prods = [
            1.5 * eye - 0.5 * folded(left_form(z), right_form(y)) for z, y in zip(zmats, ymats)
        ]
        if step == NS_STEPS - 1:
            zmats = [folded(left_form(z), right_form(p)) for z, p in zip(zmats, prods)]
        else:
            news = [
                folded(left_form(jnp.concatenate([y, z], axis=0)), right_form(p))
                for y, z, p in zip(ymats, zmats, prods)
            ]
            ymats = [new[:WIDE] for new in news]
            zmats = [new[WIDE:] for new in news]
    return [z * a * b for z, (a, b) in zip(zmats, outer)]


def turn_kernel(order_ref, gram_ref, kept_ref, arrived_ref, stay_ref, move_ref, high_ref, low_ref):
    spread(kept_ref, arrived_ref, high_ref, low_ref)
    count = kept_ref.shape[0]
    turns = turned([gram_ref[k] for k in range(count)])
    for k in range(count):
        first, second = order_ref[2 * k], order_ref[2 * k + 1]
        high = jnp.concatenate([high_ref[first], high_ref[second]], axis=0)
        low = jnp.concatenate([low_ref[first], low_ref[second]], axis=0)
        left = left_form(turns[k])
        out = jnp.dot(
            left, jnp.concatenate([high, high], axis=0), preferred_element_type=jnp.float32
        ) + jnp.dot(left, jnp.concatenate([low, low], axis=0), preferred_element_type=jnp.float32)
        stay_ref[k] = out[:BLK]
        move_ref[k] = out[BLK:]


def body(snapshots, pairing):
    rows, columns = snapshots.shape
    slots = pairing.shape[2]
    count = slots // 2
    share = lax.axis_size("rows")
    part = count * WIDE // share
    ring = lax.axis_size("pairs")
    along = [(source, (source + 1) % ring) for source in range(ring)]
    blocks = jax.ShapeDtypeStruct((count, BLK, rows), jnp.float32)
    scratch = [pltpu.VMEM((slots, BLK, rows), jnp.bfloat16)] * 2

    current = snapshots.T.reshape(count, 2, BLK, rows)
    kept, arrived = current[:, 0], current[:, 1]
    for step in range(ROUNDS):
        order = pairing[step, 0]
        gram = pl.pallas_call(
            gram_kernel,
            out_shape=jax.ShapeDtypeStruct((count, WIDE, WIDE), jnp.float32),
            in_specs=[SMEM, VMEM, VMEM],
            out_specs=VMEM,
            scratch_shapes=scratch,
        )(order, kept, arrived)
        parts = lax.all_to_all(gram.reshape(share, part, WIDE), "rows", 0, 0, tiled=True)
        copies = pl.pallas_call(
            total_kernel,
            out_shape=jax.ShapeDtypeStruct((share, part, WIDE), jnp.float32),
            in_specs=[VMEM],
            out_specs=VMEM,
        )(parts)
        gram = lax.all_to_all(copies, "rows", 0, 0, tiled=True).reshape(count, WIDE, WIDE)
        kept, moving = pl.pallas_call(
            turn_kernel,
            out_shape=(blocks, blocks),
            in_specs=[SMEM, VMEM, VMEM, VMEM],
            out_specs=(VMEM, VMEM),
            scratch_shapes=scratch,
        )(order, gram, kept, arrived)
        arrived = lax.ppermute(moving, "pairs", along)
    current = jnp.stack([kept, arrived], axis=1)
    return current.reshape(columns, rows).T


def solution(mesh):
    placed = (P("rows", "pairs"), P(None, "pairs", None))
    return jax.shard_map(
        body, mesh=mesh, in_specs=placed, out_specs=P("rows", "pairs"), check_vma=False
    )
```

```python
import functools

import jax
import jax.numpy as jnp
from jax import lax
from jax.experimental import pallas as pl
from jax.experimental.pallas import tpu as pltpu
from jax.sharding import PartitionSpec as P

BLK = 64
WIDE = 2 * BLK
ROUNDS = 5
NS_STEPS = 6

VMEM = pl.BlockSpec(memory_space=pltpu.VMEM)
SMEM = pl.BlockSpec(memory_space=pltpu.SMEM)


def halves(x):
    high = x.astype(jnp.bfloat16)
    low = (x - high.astype(jnp.float32)).astype(jnp.bfloat16)
    return high, low


def left_form(x):
    return jnp.concatenate(halves(x), axis=1)


def right_form(x):
    row = jnp.concatenate(halves(x), axis=1)
    return jnp.concatenate([row, row], axis=0)


def folded(left, right):
    out = jnp.dot(left, right, preferred_element_type=jnp.float32)
    half = out.shape[1] // 2
    return out[:, :half] + out[:, half:]


def joined(k, high_ref, low_ref):
    both = slice(2 * k, 2 * k + 2)
    rows = high_ref.shape[2]
    return jnp.concatenate(
        [high_ref[both].reshape(WIDE, rows), low_ref[both].reshape(WIDE, rows)], axis=0
    )


def times(turn, both):
    high, low = halves(turn)
    left = jnp.concatenate(
        [jnp.concatenate([high, high], axis=1), jnp.concatenate([low, low], axis=1)], axis=0
    )
    out = jnp.dot(left, both, preferred_element_type=jnp.float32)
    return out[:BLK] + out[BLK:]


def places():
    row = lax.broadcasted_iota(jnp.int32, (BLK, WIDE), 0)
    lane = lax.broadcasted_iota(jnp.int32, (BLK, WIDE), 1)
    return row, lane


def packed(gram):
    row, lane = places()
    top, bottom = gram[:BLK], gram[BLK:]
    diag = jnp.sum(jnp.where(row == lane, top, 0.0), axis=0, keepdims=True) + jnp.sum(
        jnp.where(row + BLK == lane, bottom, 0.0), axis=0, keepdims=True
    )
    return jnp.where(row > lane, pltpu.roll(bottom, BLK, 1), top), diag


def unpacked(main, diag):
    row, lane = places()
    flipped = main.T
    flipped = jnp.concatenate([flipped[:BLK], flipped[BLK:]], axis=1)
    top = jnp.where(row > lane, flipped, main)
    under = (lane >= BLK) & (row + BLK > lane)
    bottom = jnp.where(under, pltpu.roll(main, BLK, 1), pltpu.roll(flipped, BLK, 1))
    bottom = jnp.where(row + BLK == lane, diag, bottom)
    return jnp.concatenate([top, bottom], axis=0)


def write_grams(high_ref, low_ref, sums_ref):
    count = high_ref.shape[0] // 2
    sums_ref[count * BLK :] = jnp.zeros_like(sums_ref[count * BLK :])
    for k in range(count):
        both = joined(k, high_ref, low_ref)
        out = lax.dot_general(
            both[:WIDE], both, (((1,), (1,)), ((), ())), preferred_element_type=jnp.float32
        )
        cross = out[:, WIDE:]
        main, diag = packed(out[:, :WIDE] + (cross + cross.T))
        sums_ref[k * BLK : (k + 1) * BLK] = main
        sums_ref[count * BLK + k : count * BLK + k + 1] = diag


def seats(step, order_ref, seat_ref):
    for place in range(order_ref.shape[2]):
        seat_ref[order_ref[step, 0, place]] = place


def open_kernel(order_ref, block_ref, high_ref, low_ref, sums_ref, seat_ref):
    seats(0, order_ref, seat_ref)
    turned_block = block_ref[...].T
    for slot in range(high_ref.shape[0]):
        seat = seat_ref[slot]
        high_ref[seat], low_ref[seat] = halves(turned_block[slot * BLK : (slot + 1) * BLK])
    write_grams(high_ref, low_ref, sums_ref)


def gram_kernel(
    step, order_ref, kept_high, kept_low, arrived_ref, high_ref, low_ref, sums_ref, seat_ref
):
    seats(step, order_ref, seat_ref)
    for k in range(arrived_ref.shape[0]):
        seat = seat_ref[2 * k]
        high_ref[seat], low_ref[seat] = kept_high[k], kept_low[k]
        seat = seat_ref[2 * k + 1]
        high_ref[seat], low_ref[seat] = halves(arrived_ref[k])
    write_grams(high_ref, low_ref, sums_ref)


def four(a, b, c, d):
    return (a + b) + (c + d)


def turned(gram):
    row = lax.broadcasted_iota(jnp.int32, (WIDE, WIDE), 0)
    col = lax.broadcasted_iota(jnp.int32, (WIDE, WIDE), 1)
    on_diag = row == col
    eye = on_diag.astype(jnp.float32)
    ymats, zmats, outer = [], [], []
    for g in gram:
        only = jnp.where(on_diag, g, 0.0)
        diag_col = jnp.sum(only, axis=1, keepdims=True) + 1e-06
        diag_row = jnp.sum(only, axis=0, keepdims=True) + 1e-06
        scale_row = lax.rsqrt(diag_row)
        unit = g * lax.rsqrt(diag_col) * scale_row
        bound = jnp.max(jnp.sum(jnp.abs(unit), axis=1, keepdims=True), axis=0, keepdims=True)
        ymats.append(unit / bound)
        outer.append((jnp.sqrt(diag_col) * lax.rsqrt(bound), scale_row))
    for step in range(NS_STEPS):
        if step == 0:
            prods = [1.5 * eye - 0.5 * y for y in ymats]
            ymats = [folded(left_form(y), right_form(p)) for y, p in zip(ymats, prods)]
            zmats = prods
            continue
        prods = [
            1.5 * eye - 0.5 * folded(left_form(z), right_form(y)) for z, y in zip(zmats, ymats)
        ]
        if step == NS_STEPS - 1:
            zmats = [folded(left_form(z), right_form(p)) for z, p in zip(zmats, prods)]
        else:
            news = [
                folded(left_form(jnp.concatenate([y, z], axis=0)), right_form(p))
                for y, z, p in zip(ymats, zmats, prods)
            ]
            ymats = [new[:WIDE] for new in news]
            zmats = [new[WIDE:] for new in news]
    return [z * a * b for z, (a, b) in zip(zmats, outer)]


def move_kernel(high_ref, low_ref, sums_ref, move_ref, first_ref):
    count = move_ref.shape[0]
    grams = [
        unpacked(
            sums_ref[k * BLK : (k + 1) * BLK], sums_ref[count * BLK + k : count * BLK + k + 1]
        )
        for k in range(count)
    ]
    for k, turn in enumerate(turned(grams)):
        first_ref[k] = turn[:BLK]
        move_ref[k] = times(turn[BLK:], joined(k, high_ref, low_ref))


def stay_kernel(high_ref, low_ref, first_ref, kept_high, kept_low):
    for k in range(first_ref.shape[0]):
        kept_high[k], kept_low[k] = halves(times(first_ref[k], joined(k, high_ref, low_ref)))


def last_stay_kernel(high_ref, low_ref, first_ref, kept_ref):
    for k in range(first_ref.shape[0]):
        kept_ref[k] = times(first_ref[k], joined(k, high_ref, low_ref))


def close_kernel(kept_ref, arrived_ref, out_ref):
    for k in range(kept_ref.shape[0]):
        pair = jnp.concatenate([kept_ref[k], arrived_ref[k]], axis=0)
        out_ref[:, k * WIDE : (k + 1) * WIDE] = pair.T


def call(kernel, shapes, *operands, scratch=()):
    return pl.pallas_call(
        kernel,
        out_shape=shapes,
        in_specs=[SMEM if x.dtype == jnp.int32 else VMEM for x in operands],
        out_specs=jax.tree.map(lambda _: VMEM, shapes),
        scratch_shapes=scratch,
    )(*operands)


def along_y(r, d):
    return (r // 4 ^ d) * 4 + r % 4


def along_z(r, d):
    return r ^ d


def from_four(value, other):
    rows = range(lax.axis_size("rows"))
    return [value] + [
        lax.ppermute(value, "rows", [(r, other(r, d)) for r in rows]) for d in (1, 2, 3)
    ]


def body(snapshots, pairing):
    rows, columns = snapshots.shape
    slots = pairing.shape[2]
    count = slots // 2
    ring = lax.axis_size("pairs")
    along = [(source, (source + 1) % ring) for source in range(ring)]

    def of(dtype, *shape):
        return jax.ShapeDtypeStruct(shape, dtype)

    split = (of(jnp.bfloat16, slots, BLK, rows),) * 2
    half = of(jnp.float32, count, BLK, rows)
    half_split = (of(jnp.bfloat16, count, BLK, rows),) * 2
    sums = of(jnp.float32, count * BLK + 8, WIDE)
    turn = of(jnp.float32, count, BLK, WIDE)

    seat = [pltpu.SMEM((slots,), jnp.int32)]
    high, low, gram = call(open_kernel, (*split, sums), pairing, snapshots, scratch=seat)
    for step in range(ROUNDS):
        part = four(*from_four(gram, along_y))
        total = four(*from_four(part, along_z))
        move, first = call(move_kernel, (half, turn), high, low, total)
        arrived = lax.ppermute(move, "pairs", along)
        if step == ROUNDS - 1:
            kept = call(last_stay_kernel, half, high, low, first)
            return call(close_kernel, of(jnp.float32, rows, columns), kept, arrived)
        kept = call(stay_kernel, half_split, high, low, first)
        high, low, gram = call(
            functools.partial(gram_kernel, step + 1),
            (*split, sums),
            pairing,
            *kept,
            arrived,
            scratch=seat,
        )


def solution(mesh):
    placed = (P("rows", "pairs"), P(None, "pairs", None))
    return jax.shard_map(
        body, mesh=mesh, in_specs=placed, out_specs=P("rows", "pairs"), check_vma=False
    )
```

```python
import functools

import jax
import jax.numpy as jnp
from jax import lax
from jax.experimental import pallas as pl
from jax.experimental.pallas import tpu as pltpu
from jax.sharding import PartitionSpec as P

BLK = 64
WIDE = 2 * BLK
ROUNDS = 5
NS_STEPS = 6
ROOM = 16 << 20

VMEM = pl.BlockSpec(memory_space=pltpu.VMEM)
SMEM = pl.BlockSpec(memory_space=pltpu.SMEM)


def halves(x):
    high = x.astype(jnp.bfloat16)
    low = (x - high.astype(jnp.float32)).astype(jnp.bfloat16)
    return high, low


def left_form(x):
    return jnp.concatenate(halves(x), axis=1)


def right_form(x):
    row = jnp.concatenate(halves(x), axis=1)
    return jnp.concatenate([row, row], axis=0)


def folded(left, right):
    out = jnp.dot(left, right, preferred_element_type=jnp.float32)
    half = out.shape[1] // 2
    return out[:, :half] + out[:, half:]


def joined(k, high_ref, low_ref):
    both = slice(2 * k, 2 * k + 2)
    rows = high_ref.shape[2]
    return jnp.concatenate(
        [high_ref[both].reshape(WIDE, rows), low_ref[both].reshape(WIDE, rows)], axis=0
    )


def times(turn, both):
    high, low = halves(turn)
    left = jnp.concatenate(
        [jnp.concatenate([high, high], axis=1), jnp.concatenate([low, low], axis=1)], axis=0
    )
    out = jnp.dot(left, both, preferred_element_type=jnp.float32)
    return out[:BLK] + out[BLK:]


def places():
    row = lax.broadcasted_iota(jnp.int32, (BLK, WIDE), 0)
    lane = lax.broadcasted_iota(jnp.int32, (BLK, WIDE), 1)
    return row, lane


def packed(gram):
    row, lane = places()
    top, bottom = gram[:BLK], gram[BLK:]
    diag = jnp.sum(jnp.where(row == lane, top, 0.0), axis=0, keepdims=True) + jnp.sum(
        jnp.where(row + BLK == lane, bottom, 0.0), axis=0, keepdims=True
    )
    return jnp.where(row > lane, pltpu.roll(bottom, BLK, 1), top), diag


def unpacked(main, diag):
    row, lane = places()
    flipped = main.T
    flipped = jnp.concatenate([flipped[:BLK], flipped[BLK:]], axis=1)
    top = jnp.where(row > lane, flipped, main)
    under = (lane >= BLK) & (row + BLK > lane)
    bottom = jnp.where(under, pltpu.roll(main, BLK, 1), pltpu.roll(flipped, BLK, 1))
    bottom = jnp.where(row + BLK == lane, diag, bottom)
    return jnp.concatenate([top, bottom], axis=0)


def write_grams(high_ref, low_ref, sums_ref):
    count = high_ref.shape[0] // 2
    sums_ref[count * BLK :] = jnp.zeros_like(sums_ref[count * BLK :])
    for k in range(count):
        both = joined(k, high_ref, low_ref)
        out = lax.dot_general(
            both[:WIDE], both, (((1,), (1,)), ((), ())), preferred_element_type=jnp.float32
        )
        cross = out[:, WIDE:]
        main, diag = packed(out[:, :WIDE] + (cross + cross.T))
        sums_ref[k * BLK : (k + 1) * BLK] = main
        sums_ref[count * BLK + k : count * BLK + k + 1] = diag


def seats(step, order_ref, seat_ref):
    for place in range(order_ref.shape[2]):
        seat_ref[order_ref[step, 0, place]] = place


def open_kernel(order_ref, block_ref, high_ref, low_ref, sums_ref, seat_ref):
    seats(0, order_ref, seat_ref)
    turned_block = block_ref[...].T
    for slot in range(high_ref.shape[0]):
        seat = seat_ref[slot]
        high_ref[seat], low_ref[seat] = halves(turned_block[slot * BLK : (slot + 1) * BLK])
    write_grams(high_ref, low_ref, sums_ref)


def gram_kernel(
    step, order_ref, kept_high, kept_low, arrived_ref, high_ref, low_ref, sums_ref, seat_ref
):
    seats(step, order_ref, seat_ref)
    for k in range(arrived_ref.shape[0]):
        seat = seat_ref[2 * k]
        high_ref[seat], low_ref[seat] = kept_high[k], kept_low[k]
        seat = seat_ref[2 * k + 1]
        high_ref[seat], low_ref[seat] = halves(arrived_ref[k])
    write_grams(high_ref, low_ref, sums_ref)


def four(a, b, c, d):
    return (a + b) + (c + d)


def turned(gram):
    row = lax.broadcasted_iota(jnp.int32, (WIDE, WIDE), 0)
    col = lax.broadcasted_iota(jnp.int32, (WIDE, WIDE), 1)
    on_diag = row == col
    eye = on_diag.astype(jnp.float32)
    ymats, zmats, outer = [], [], []
    for g in gram:
        only = jnp.where(on_diag, g, 0.0)
        diag_col = jnp.sum(only, axis=1, keepdims=True) + 1e-06
        diag_row = jnp.sum(only, axis=0, keepdims=True) + 1e-06
        scale_row = lax.rsqrt(diag_row)
        unit = g * lax.rsqrt(diag_col) * scale_row
        bound = jnp.max(jnp.sum(jnp.abs(unit), axis=1, keepdims=True), axis=0, keepdims=True)
        ymats.append(unit / bound)
        outer.append((jnp.sqrt(diag_col) * lax.rsqrt(bound), scale_row))
    for step in range(NS_STEPS):
        if step == 0:
            prods = [1.5 * eye - 0.5 * y for y in ymats]
            ymats = [folded(left_form(y), right_form(p)) for y, p in zip(ymats, prods)]
            zmats = prods
            continue
        prods = [
            1.5 * eye - 0.5 * folded(left_form(z), right_form(y)) for z, y in zip(zmats, ymats)
        ]
        if step == NS_STEPS - 1:
            zmats = [folded(left_form(z), right_form(p)) for z, p in zip(zmats, prods)]
        else:
            news = [
                folded(left_form(jnp.concatenate([y, z], axis=0)), right_form(p))
                for y, z, p in zip(ymats, zmats, prods)
            ]
            ymats = [new[:WIDE] for new in news]
            zmats = [new[WIDE:] for new in news]
    return [z * a * b for z, (a, b) in zip(zmats, outer)]


def move_kernel(high_ref, low_ref, sums_ref, move_ref, first_ref):
    count = move_ref.shape[0]
    grams = [
        unpacked(
            sums_ref[k * BLK : (k + 1) * BLK], sums_ref[count * BLK + k : count * BLK + k + 1]
        )
        for k in range(count)
    ]
    for k, turn in enumerate(turned(grams)):
        first_ref[k] = turn[:BLK]
        move_ref[k] = times(turn[BLK:], joined(k, high_ref, low_ref))


def stay_kernel(high_ref, low_ref, first_ref, kept_high, kept_low):
    for k in range(first_ref.shape[0]):
        kept_high[k], kept_low[k] = halves(times(first_ref[k], joined(k, high_ref, low_ref)))


def last_stay_kernel(high_ref, low_ref, first_ref, kept_ref):
    for k in range(first_ref.shape[0]):
        kept_ref[k] = times(first_ref[k], joined(k, high_ref, low_ref))


def close_kernel(kept_ref, arrived_ref, out_ref):
    for k in range(kept_ref.shape[0]):
        pair = jnp.concatenate([kept_ref[k], arrived_ref[k]], axis=0)
        out_ref[:, k * WIDE : (k + 1) * WIDE] = pair.T


def call(kernel, shapes, *operands, scratch=()):
    return pl.pallas_call(
        kernel,
        out_shape=shapes,
        in_specs=[SMEM if x.dtype == jnp.int32 else VMEM for x in operands],
        out_specs=jax.tree.map(lambda _: VMEM, shapes),
        scratch_shapes=scratch,
        compiler_params=pltpu.CompilerParams(vmem_limit_bytes=ROOM),
    )(*operands)


def along_y(r, d):
    return (r // 4 ^ d) * 4 + r % 4


def along_z(r, d):
    return r ^ d


def from_four(value, other):
    rows = range(lax.axis_size("rows"))
    return [value] + [
        lax.ppermute(value, "rows", [(r, other(r, d)) for r in rows]) for d in (1, 2, 3)
    ]


def body(snapshots, pairing):
    rows, columns = snapshots.shape
    slots = pairing.shape[2]
    count = slots // 2
    ring = lax.axis_size("pairs")
    along = [(source, (source + 1) % ring) for source in range(ring)]

    def of(dtype, *shape):
        return jax.ShapeDtypeStruct(shape, dtype)

    split = (of(jnp.bfloat16, slots, BLK, rows),) * 2
    half = of(jnp.float32, count, BLK, rows)
    half_split = (of(jnp.bfloat16, count, BLK, rows),) * 2
    sums = of(jnp.float32, count * BLK + 8, WIDE)
    turn = of(jnp.float32, count, BLK, WIDE)

    seat = [pltpu.SMEM((slots,), jnp.int32)]
    high, low, gram = call(open_kernel, (*split, sums), pairing, snapshots, scratch=seat)
    for step in range(ROUNDS):
        part = four(*from_four(gram, along_y))
        total = four(*from_four(part, along_z))
        move, first = call(move_kernel, (half, turn), high, low, total)
        arrived = lax.ppermute(move, "pairs", along)
        if step == ROUNDS - 1:
            kept = call(last_stay_kernel, half, high, low, first)
            return call(close_kernel, of(jnp.float32, rows, columns), kept, arrived)
        kept = call(stay_kernel, half_split, high, low, first)
        high, low, gram = call(
            functools.partial(gram_kernel, step + 1),
            (*split, sums),
            pairing,
            *kept,
            arrived,
            scratch=seat,
        )


def solution(mesh):
    placed = (P("rows", "pairs"), P(None, "pairs", None))
    return jax.shard_map(
        body, mesh=mesh, in_specs=placed, out_specs=P("rows", "pairs"), check_vma=False
    )
```

```python
import functools

import jax
import jax.numpy as jnp
from jax import lax
from jax.experimental import pallas as pl
from jax.experimental.pallas import tpu as pltpu
from jax.sharding import PartitionSpec as P

BLK = 64
WIDE = 2 * BLK
ROUNDS = 5
NS_STEPS = 6
ROOM = 16 << 20
WHOLE = 60 << 20

VMEM = pl.BlockSpec(memory_space=pltpu.VMEM)
SMEM = pl.BlockSpec(memory_space=pltpu.SMEM)
FAR = pl.BlockSpec(memory_space=pltpu.HBM)


def halves(x):
    high = x.astype(jnp.bfloat16)
    low = (x - high.astype(jnp.float32)).astype(jnp.bfloat16)
    return high, low


def left_form(x):
    return jnp.concatenate(halves(x), axis=1)


def right_form(x):
    row = jnp.concatenate(halves(x), axis=1)
    return jnp.concatenate([row, row], axis=0)


def folded(left, right):
    out = jnp.dot(left, right, preferred_element_type=jnp.float32)
    half = out.shape[1] // 2
    return out[:, :half] + out[:, half:]


def joined(k, high_ref, low_ref):
    both = slice(2 * k, 2 * k + 2)
    rows = high_ref.shape[2]
    return jnp.concatenate(
        [high_ref[both].reshape(WIDE, rows), low_ref[both].reshape(WIDE, rows)], axis=0
    )


def times(turn, both):
    high, low = halves(turn)
    left = jnp.concatenate(
        [jnp.concatenate([high, high], axis=1), jnp.concatenate([low, low], axis=1)], axis=0
    )
    out = jnp.dot(left, both, preferred_element_type=jnp.float32)
    return out[:BLK] + out[BLK:]


def places():
    row = lax.broadcasted_iota(jnp.int32, (BLK, WIDE), 0)
    lane = lax.broadcasted_iota(jnp.int32, (BLK, WIDE), 1)
    return row, lane


def packed(gram):
    row, lane = places()
    top, bottom = gram[:BLK], gram[BLK:]
    diag = jnp.sum(jnp.where(row == lane, top, 0.0), axis=0, keepdims=True) + jnp.sum(
        jnp.where(row + BLK == lane, bottom, 0.0), axis=0, keepdims=True
    )
    return jnp.where(row > lane, pltpu.roll(bottom, BLK, 1), top), diag


def unpacked(main, diag):
    row, lane = places()
    flipped = main.T
    flipped = jnp.concatenate([flipped[:BLK], flipped[BLK:]], axis=1)
    top = jnp.where(row > lane, flipped, main)
    under = (lane >= BLK) & (row + BLK > lane)
    bottom = jnp.where(under, pltpu.roll(main, BLK, 1), pltpu.roll(flipped, BLK, 1))
    bottom = jnp.where(row + BLK == lane, diag, bottom)
    return jnp.concatenate([top, bottom], axis=0)


def write_grams(high_ref, low_ref, sums_ref):
    count = high_ref.shape[0] // 2
    sums_ref[count * BLK :] = jnp.zeros_like(sums_ref[count * BLK :])
    for k in range(count):
        both = joined(k, high_ref, low_ref)
        out = lax.dot_general(
            both[:WIDE], both, (((1,), (1,)), ((), ())), preferred_element_type=jnp.float32
        )
        cross = out[:, WIDE:]
        main, diag = packed(out[:, :WIDE] + (cross + cross.T))
        sums_ref[k * BLK : (k + 1) * BLK] = main
        sums_ref[count * BLK + k : count * BLK + k + 1] = diag


def seats(step, order_ref, seat_ref):
    for place in range(order_ref.shape[2]):
        seat_ref[order_ref[step, 0, place]] = place


def open_kernel(order_ref, block_ref, high_ref, low_ref, sums_ref, seat_ref, buffer, sems):
    copies = [
        pltpu.make_async_copy(
            block_ref.at[:, k * WIDE : (k + 1) * WIDE], buffer.at[k], sems.at[k]
        )
        for k in range(buffer.shape[0])
    ]
    for copy in copies:
        copy.start()
    seats(0, order_ref, seat_ref)
    for k, copy in enumerate(copies):
        copy.wait()
        turned_block = buffer[k].T
        for side in range(2):
            seat = seat_ref[2 * k + side]
            high_ref[seat], low_ref[seat] = halves(turned_block[side * BLK : (side + 1) * BLK])
    write_grams(high_ref, low_ref, sums_ref)


def gram_kernel(
    step, order_ref, kept_high, kept_low, arrived_ref, high_ref, low_ref, sums_ref, seat_ref
):
    seats(step, order_ref, seat_ref)
    for k in range(arrived_ref.shape[0]):
        seat = seat_ref[2 * k]
        high_ref[seat], low_ref[seat] = kept_high[k], kept_low[k]
        seat = seat_ref[2 * k + 1]
        high_ref[seat], low_ref[seat] = halves(arrived_ref[k])
    write_grams(high_ref, low_ref, sums_ref)


def four(a, b, c, d):
    return (a + b) + (c + d)


def turned(gram):
    row = lax.broadcasted_iota(jnp.int32, (WIDE, WIDE), 0)
    col = lax.broadcasted_iota(jnp.int32, (WIDE, WIDE), 1)
    on_diag = row == col
    eye = on_diag.astype(jnp.float32)
    ymats, zmats, outer = [], [], []
    for g in gram:
        only = jnp.where(on_diag, g, 0.0)
        diag_col = jnp.sum(only, axis=1, keepdims=True) + 1e-06
        diag_row = jnp.sum(only, axis=0, keepdims=True) + 1e-06
        scale_row = lax.rsqrt(diag_row)
        unit = g * lax.rsqrt(diag_col) * scale_row
        bound = jnp.max(jnp.sum(jnp.abs(unit), axis=1, keepdims=True), axis=0, keepdims=True)
        ymats.append(unit / bound)
        outer.append((jnp.sqrt(diag_col) * lax.rsqrt(bound), scale_row))
    for step in range(NS_STEPS):
        if step == 0:
            prods = [1.5 * eye - 0.5 * y for y in ymats]
            ymats = [folded(left_form(y), right_form(p)) for y, p in zip(ymats, prods)]
            zmats = prods
            continue
        prods = [
            1.5 * eye - 0.5 * folded(left_form(z), right_form(y)) for z, y in zip(zmats, ymats)
        ]
        if step == NS_STEPS - 1:
            zmats = [folded(left_form(z), right_form(p)) for z, p in zip(zmats, prods)]
        else:
            news = [
                folded(left_form(jnp.concatenate([y, z], axis=0)), right_form(p))
                for y, z, p in zip(ymats, zmats, prods)
            ]
            ymats = [new[:WIDE] for new in news]
            zmats = [new[WIDE:] for new in news]
    return [z * a * b for z, (a, b) in zip(zmats, outer)]


def move_kernel(high_ref, low_ref, sums_ref, move_ref, first_ref):
    count = move_ref.shape[0]
    grams = [
        unpacked(
            sums_ref[k * BLK : (k + 1) * BLK], sums_ref[count * BLK + k : count * BLK + k + 1]
        )
        for k in range(count)
    ]
    for k, turn in enumerate(turned(grams)):
        first_ref[k] = turn[:BLK]
        move_ref[k] = times(turn[BLK:], joined(k, high_ref, low_ref))


def stay_kernel(high_ref, low_ref, first_ref, kept_high, kept_low):
    for k in range(first_ref.shape[0]):
        kept_high[k], kept_low[k] = halves(times(first_ref[k], joined(k, high_ref, low_ref)))


def last_stay_kernel(high_ref, low_ref, first_ref, kept_ref):
    for k in range(first_ref.shape[0]):
        kept_ref[k] = times(first_ref[k], joined(k, high_ref, low_ref))


def close_kernel(kept_ref, arrived_ref, out_ref, buffer, sems):
    copies = []
    for k in range(kept_ref.shape[0]):
        buffer[k] = jnp.concatenate([kept_ref[k], arrived_ref[k]], axis=0).T
        copies.append(
            pltpu.make_async_copy(
                buffer.at[k], out_ref.at[:, k * WIDE : (k + 1) * WIDE], sems.at[k]
            )
        )
        copies[-1].start()
    for copy in copies:
        copy.wait()


def call(kernel, shapes, *operands, scratch=(), far_in=(), far_out=False, room=ROOM):
    ends = [SMEM if x.dtype == jnp.int32 else VMEM for x in operands] + [FAR] * len(far_in)
    return pl.pallas_call(
        kernel,
        out_shape=shapes,
        in_specs=ends,
        out_specs=jax.tree.map(lambda _: FAR if far_out else VMEM, shapes),
        scratch_shapes=scratch,
        compiler_params=pltpu.CompilerParams(vmem_limit_bytes=room),
    )(*operands, *far_in)


def along_y(r, d):
    return (r // 4 ^ d) * 4 + r % 4


def along_z(r, d):
    return r ^ d


def from_four(value, other):
    rows = range(lax.axis_size("rows"))
    return [value] + [
        lax.ppermute(value, "rows", [(r, other(r, d)) for r in rows]) for d in (1, 2, 3)
    ]


def body(snapshots, pairing):
    rows, columns = snapshots.shape
    slots = pairing.shape[2]
    count = slots // 2
    ring = lax.axis_size("pairs")
    along = [(source, (source + 1) % ring) for source in range(ring)]

    def of(dtype, *shape):
        return jax.ShapeDtypeStruct(shape, dtype)

    split = (of(jnp.bfloat16, slots, BLK, rows),) * 2
    half = of(jnp.float32, count, BLK, rows)
    half_split = (of(jnp.bfloat16, count, BLK, rows),) * 2
    sums = of(jnp.float32, count * BLK + 8, WIDE)
    turn = of(jnp.float32, count, BLK, WIDE)

    seat = [pltpu.SMEM((slots,), jnp.int32)]
    chunks = [pltpu.VMEM((count, rows, WIDE), jnp.float32), pltpu.SemaphoreType.DMA((count,))]
    high, low, gram = call(
        open_kernel,
        (*split, sums),
        pairing,
        scratch=seat + chunks,
        far_in=(snapshots,),
        room=WHOLE,
    )
    for step in range(ROUNDS):
        part = four(*from_four(gram, along_y))
        total = four(*from_four(part, along_z))
        move, first = call(move_kernel, (half, turn), high, low, total)
        arrived = lax.ppermute(move, "pairs", along)
        if step == ROUNDS - 1:
            kept = call(last_stay_kernel, half, high, low, first)
            out = of(jnp.float32, rows, columns)
            return call(close_kernel, out, kept, arrived, scratch=chunks, far_out=True)
        kept = call(stay_kernel, half_split, high, low, first)
        high, low, gram = call(
            functools.partial(gram_kernel, step + 1),
            (*split, sums),
            pairing,
            *kept,
            arrived,
            scratch=seat,
        )


def solution(mesh):
    placed = (P("rows", "pairs"), P(None, "pairs", None))
    return jax.shard_map(
        body, mesh=mesh, in_specs=placed, out_specs=P("rows", "pairs"), check_vma=False
    )
```

```python
import functools

import jax
import jax.numpy as jnp
from jax import lax
from jax.experimental import pallas as pl
from jax.experimental.pallas import tpu as pltpu
from jax.sharding import PartitionSpec as P

BLK = 64
WIDE = 2 * BLK
ROUNDS = 5
NS_STEPS = 6
ROOM = 16 << 20

VMEM = pl.BlockSpec(memory_space=pltpu.VMEM)
SMEM = pl.BlockSpec(memory_space=pltpu.SMEM)


def halves(x):
    high = x.astype(jnp.bfloat16)
    low = (x - high.astype(jnp.float32)).astype(jnp.bfloat16)
    return high, low


def left_form(x):
    return jnp.concatenate(halves(x), axis=1)


def right_form(x):
    row = jnp.concatenate(halves(x), axis=1)
    return jnp.concatenate([row, row], axis=0)


def folded(left, right):
    out = jnp.dot(left, right, preferred_element_type=jnp.float32)
    half = out.shape[1] // 2
    return out[:, :half] + out[:, half:]


def joined(k, high_ref, low_ref):
    both = slice(2 * k, 2 * k + 2)
    rows = high_ref.shape[2]
    return jnp.concatenate(
        [high_ref[both].reshape(WIDE, rows), low_ref[both].reshape(WIDE, rows)], axis=0
    )


def times(turn, both):
    high, low = halves(turn)
    left = jnp.concatenate(
        [jnp.concatenate([high, high], axis=1), jnp.concatenate([low, low], axis=1)], axis=0
    )
    out = jnp.dot(left, both, preferred_element_type=jnp.float32)
    return out[:BLK] + out[BLK:]


def places():
    row = lax.broadcasted_iota(jnp.int32, (BLK, WIDE), 0)
    lane = lax.broadcasted_iota(jnp.int32, (BLK, WIDE), 1)
    return row, lane


def packed(gram):
    row, lane = places()
    top, bottom = gram[:BLK], gram[BLK:]
    diag = jnp.sum(jnp.where(row == lane, top, 0.0), axis=0, keepdims=True) + jnp.sum(
        jnp.where(row + BLK == lane, bottom, 0.0), axis=0, keepdims=True
    )
    return jnp.where(row > lane, pltpu.roll(bottom, BLK, 1), top), diag


def unpacked(main, diag):
    row, lane = places()
    flipped = main.T
    flipped = jnp.concatenate([flipped[:BLK], flipped[BLK:]], axis=1)
    top = jnp.where(row > lane, flipped, main)
    under = (lane >= BLK) & (row + BLK > lane)
    bottom = jnp.where(under, pltpu.roll(main, BLK, 1), pltpu.roll(flipped, BLK, 1))
    bottom = jnp.where(row + BLK == lane, diag, bottom)
    return jnp.concatenate([top, bottom], axis=0)


def write_grams(high_ref, low_ref, sums_ref):
    count = high_ref.shape[0] // 2
    sums_ref[count * BLK :] = jnp.zeros_like(sums_ref[count * BLK :])
    for k in range(count):
        both = joined(k, high_ref, low_ref)
        out = lax.dot_general(
            both[:WIDE], both, (((1,), (1,)), ((), ())), preferred_element_type=jnp.float32
        )
        cross = out[:, WIDE:]
        main, diag = packed(out[:, :WIDE] + (cross + cross.T))
        sums_ref[k * BLK : (k + 1) * BLK] = main
        sums_ref[count * BLK + k : count * BLK + k + 1] = diag


def seats(step, order_ref, seat_ref):
    for place in range(order_ref.shape[2]):
        seat_ref[order_ref[step, 0, place]] = place


def open_kernel(order_ref, block_ref, high_ref, low_ref, sums_ref, seat_ref):
    seats(0, order_ref, seat_ref)
    turned_block = block_ref[...].T
    for slot in range(high_ref.shape[0]):
        seat = seat_ref[slot]
        high_ref[seat], low_ref[seat] = halves(turned_block[slot * BLK : (slot + 1) * BLK])
    write_grams(high_ref, low_ref, sums_ref)


def gram_kernel(
    step, order_ref, kept_high, kept_low, arrived_ref, high_ref, low_ref, sums_ref, seat_ref
):
    seats(step, order_ref, seat_ref)
    for k in range(arrived_ref.shape[0]):
        seat = seat_ref[2 * k]
        high_ref[seat], low_ref[seat] = kept_high[k], kept_low[k]
        seat = seat_ref[2 * k + 1]
        high_ref[seat], low_ref[seat] = halves(arrived_ref[k])
    write_grams(high_ref, low_ref, sums_ref)


def four(a, b, c, d):
    return (a + b) + (c + d)


def turned(gram):
    row = lax.broadcasted_iota(jnp.int32, (WIDE, WIDE), 0)
    col = lax.broadcasted_iota(jnp.int32, (WIDE, WIDE), 1)
    on_diag = row == col
    eye = on_diag.astype(jnp.float32)
    ymats, zmats, outer = [], [], []
    for g in gram:
        only = jnp.where(on_diag, g, 0.0)
        diag_col = jnp.sum(only, axis=1, keepdims=True) + 1e-06
        diag_row = jnp.sum(only, axis=0, keepdims=True) + 1e-06
        scale_row = lax.rsqrt(diag_row)
        unit = g * lax.rsqrt(diag_col) * scale_row
        bound = jnp.max(jnp.sum(jnp.abs(unit), axis=1, keepdims=True), axis=0, keepdims=True)
        ymats.append(unit / bound)
        outer.append((jnp.sqrt(diag_col) * lax.rsqrt(bound), scale_row))
    for step in range(NS_STEPS):
        if step == 0:
            prods = [1.5 * eye - 0.5 * y for y in ymats]
            ymats = [folded(left_form(y), right_form(p)) for y, p in zip(ymats, prods)]
            zmats = prods
            continue
        ylefts, zlefts = [left_form(y) for y in ymats], [left_form(z) for z in zmats]
        prods = [
            1.5 * eye - 0.5 * folded(z, jnp.concatenate([y, y], axis=0))
            for z, y in zip(zlefts, ylefts)
        ]
        if step == NS_STEPS - 1:
            zmats = [folded(z, right_form(p)) for z, p in zip(zlefts, prods)]
        else:
            news = [
                folded(jnp.concatenate([y, z], axis=0), right_form(p))
                for y, z, p in zip(ylefts, zlefts, prods)
            ]
            ymats = [new[:WIDE] for new in news]
            zmats = [new[WIDE:] for new in news]
    return [z * a * b for z, (a, b) in zip(zmats, outer)]


def move_kernel(high_ref, low_ref, sums_ref, move_ref, first_ref):
    count = move_ref.shape[0]
    grams = [
        unpacked(
            sums_ref[k * BLK : (k + 1) * BLK], sums_ref[count * BLK + k : count * BLK + k + 1]
        )
        for k in range(count)
    ]
    for k, turn in enumerate(turned(grams)):
        first_ref[k] = turn[:BLK]
        move_ref[k] = times(turn[BLK:], joined(k, high_ref, low_ref))


def stay_kernel(high_ref, low_ref, first_ref, kept_high, kept_low):
    for k in range(first_ref.shape[0]):
        kept_high[k], kept_low[k] = halves(times(first_ref[k], joined(k, high_ref, low_ref)))


def last_stay_kernel(high_ref, low_ref, first_ref, kept_ref):
    for k in range(first_ref.shape[0]):
        kept_ref[k] = times(first_ref[k], joined(k, high_ref, low_ref))


def close_kernel(kept_ref, arrived_ref, out_ref):
    for k in range(kept_ref.shape[0]):
        pair = jnp.concatenate([kept_ref[k], arrived_ref[k]], axis=0)
        out_ref[:, k * WIDE : (k + 1) * WIDE] = pair.T


def call(kernel, shapes, *operands, scratch=()):
    return pl.pallas_call(
        kernel,
        out_shape=shapes,
        in_specs=[SMEM if x.dtype == jnp.int32 else VMEM for x in operands],
        out_specs=jax.tree.map(lambda _: VMEM, shapes),
        scratch_shapes=scratch,
        compiler_params=pltpu.CompilerParams(vmem_limit_bytes=ROOM),
    )(*operands)


def along_y(r, d):
    return (r // 4 ^ d) * 4 + r % 4


def along_z(r, d):
    return r ^ d


def from_four(value, other):
    rows = range(lax.axis_size("rows"))
    return [value] + [
        lax.ppermute(value, "rows", [(r, other(r, d)) for r in rows]) for d in (1, 2, 3)
    ]


def body(snapshots, pairing):
    rows, columns = snapshots.shape
    slots = pairing.shape[2]
    count = slots // 2
    ring = lax.axis_size("pairs")
    along = [(source, (source + 1) % ring) for source in range(ring)]

    def of(dtype, *shape):
        return jax.ShapeDtypeStruct(shape, dtype)

    split = (of(jnp.bfloat16, slots, BLK, rows),) * 2
    half = of(jnp.float32, count, BLK, rows)
    half_split = (of(jnp.bfloat16, count, BLK, rows),) * 2
    sums = of(jnp.float32, count * BLK + 8, WIDE)
    turn = of(jnp.float32, count, BLK, WIDE)

    seat = [pltpu.SMEM((slots,), jnp.int32)]
    high, low, gram = call(open_kernel, (*split, sums), pairing, snapshots, scratch=seat)
    for step in range(ROUNDS):
        part = four(*from_four(gram, along_y))
        total = four(*from_four(part, along_z))
        move, first = call(move_kernel, (half, turn), high, low, total)
        arrived = lax.ppermute(move, "pairs", along)
        if step == ROUNDS - 1:
            kept = call(last_stay_kernel, half, high, low, first)
            return call(close_kernel, of(jnp.float32, rows, columns), kept, arrived)
        kept = call(stay_kernel, half_split, high, low, first)
        high, low, gram = call(
            functools.partial(gram_kernel, step + 1),
            (*split, sums),
            pairing,
            *kept,
            arrived,
            scratch=seat,
        )


def solution(mesh):
    placed = (P("rows", "pairs"), P(None, "pairs", None))
    return jax.shard_map(
        body, mesh=mesh, in_specs=placed, out_specs=P("rows", "pairs"), check_vma=False
    )
```
